512 devices in a mesh: row: 16 (over z_lo, core), col: 32 (over y, x, z_hi).
Axes of the slice: x: 4, y: 4, z: 16 (z_hi: 2, z_lo: 8; z = z_hi * 8 + z_lo), core: 2. Of those that a mesh axis runs over, the one named last changes fastest.
Arguments:
- signatures: bfloat16 [8192, 49152], P('row', 'col'), as said below
- trailing: float32 [8192, 4096], P('row', 'col'), may hold values from -6 to 6
- ridge: float32 [1], replicated, may hold values from 0.5 to 2
- panel_index: int32 [1], replicated, may hold values from 1 to 15
Outputs:
- factor: float32 [8192, 256], P(('row', 'col'))
- updated: float32 [8192, 4096], P('row', 'col')
The draws below stay inside these ranges and needn't reach their ends.
Inputs may be any that keep to these rules, and one draw needn't show every extreme that they name: `signatures`: every diagonal block of the Gram matrix plus the ridge is positive definite.
All inputs are finite; a program needn't handle non-finite values.
Results may differ from the reference program's by a relative error of at most 0.0003.
Values may be sent and summed in bfloat16 or wider, within the bound.
No kernel may reach another device: no remote copies, remote signals or barrier semaphores. Data moves between devices by JAX's collectives and lax.ppermute only.
A program may use at most 64 MiB of HBM per device.

```python
import math
import jax
import jax.numpy as jnp
from jax import lax

PANEL = 256
FEATURES = 49152
ROWS_DEV = 512
ORDER = 8192
WINDOW = 4096


def draw_signatures(key, part):
    keys = jax.random.split(jax.random.fold_in(key, 7), 6)
    noise = jax.random.normal(keys[0], (ORDER, FEATURES), jnp.float32)
    scales = jnp.exp(jax.random.uniform(keys[1], (ORDER, 1), jnp.float32, -0.7, 0.7))
    mixing = jax.random.normal(keys[2], (ORDER, PANEL), jnp.float32)
    shared = jax.random.normal(keys[3], (ORDER, 1), jnp.float32) * jax.random.normal(keys[4], (1, PANEL), jnp.float32)
    mixing = mixing + 0.7 * shared
    pattern = jax.random.normal(keys[5], (PANEL, FEATURES // PANEL), jnp.float32)
    common = (mixing[:, :, None] * pattern[None, :, :]).reshape(ORDER, FEATURES)
    values = (scales * noise + common) / jnp.sqrt(jnp.float32(FEATURES))
    return values.astype(jnp.bfloat16)


def block_levels(rng, dims, pieces, smallest, high):
    loudness, own = 1.0, jax.random.fold_in(rng, 6)
    for position, parts in pieces:
        steps = jnp.exp(jax.random.uniform(jax.random.fold_in(own, position), (parts,), jnp.float32, smallest / len(pieces), high / len(pieces)))
        loudness = loudness * jnp.repeat(steps, dims[position] // parts).reshape([-1 if axis == position else 1 for axis in range(len(dims))])
    return loudness


def normal_values(key, shape, spread, bound, pieces=(), kind=jnp.bfloat16):
    gain = block_levels(key, shape, pieces, -0.22, 0.18) if pieces else 1.0
    drawn = jax.random.normal(key, shape, jnp.float32) * spread * gain
    return jnp.minimum(jnp.maximum(drawn, -bound), bound).astype(kind)


def setup_inputs(seed: int = 0) -> dict:
    key_list = jax.random.split(jax.random.key(seed), 5)
    signatures = draw_signatures(jax.random.fold_in(key_list[4], 71), 0)
    trailing = normal_values(key_list[1], (ORDER, WINDOW), 1.0, 6.0, ((0, 16), (1, 32)), jnp.float32)
    ridge = jnp.clip(jnp.exp(jax.random.uniform(key_list[2], (1,), jnp.float32, math.log(0.5), math.log(2.0))), 0.5, 2.0)
    panel_index = jax.random.randint(key_list[3], (1,), 1, (ORDER - WINDOW) // PANEL).astype(jnp.int32)
    return dict(signatures=signatures, trailing=trailing, ridge=ridge, panel_index=panel_index)


def add_ridge(block, first_row, panel_start, ridge):
    row_ids = first_row + lax.broadcasted_iota(jnp.int32, block.shape, 0)
    col_ids = panel_start + lax.broadcasted_iota(jnp.int32, block.shape, 1)
    return block + jnp.where(row_ids == col_ids, ridge[0], jnp.zeros((), block.dtype))

def reference(signatures, trailing, ridge, panel_index):
    panel_start = (panel_index[0] * PANEL).astype(jnp.int32)
    panel_paths = lax.dynamic_slice_in_dim(signatures, panel_start, PANEL, 0)
    row_blocks = signatures.reshape(ORDER // ROWS_DEV, ROWS_DEV, FEATURES)

    def block_product(row_block):
        return lax.dot_general(row_block.astype(jnp.float32), panel_paths.astype(jnp.float32), (((1,), (1,)), ((), ())), preferred_element_type=jnp.float32)
    panel_cols = lax.map(block_product, row_blocks).reshape(ORDER, PANEL)
    panel_cols = add_ridge(panel_cols, jnp.int32(0), panel_start, ridge)
    diagonal = lax.dynamic_slice_in_dim(panel_cols, panel_start, PANEL, 0)
    lower = jnp.linalg.cholesky(diagonal)
    factor = jax.scipy.linalg.solve_triangular(lower, panel_cols.T, lower=True).T
    row_ids = lax.broadcasted_iota(jnp.int32, factor.shape, 0)
    factor = jnp.where(row_ids >= panel_start, factor, jnp.zeros((), factor.dtype))
    trailing_start = (panel_start + PANEL).astype(jnp.int32)
    window_rows = lax.dynamic_slice_in_dim(factor, trailing_start, WINDOW, 0)
    updated = trailing - lax.dot_general(factor.astype(jnp.float32), window_rows.astype(jnp.float32), (((1,), (1,)), ((), ())), precision=lax.Precision.HIGHEST, preferred_element_type=jnp.float32)
    return (factor, updated)
```

```python
import jax
import jax.numpy as jnp
from jax import lax
from jax.experimental import pallas as pl
from jax.experimental.pallas import tpu as pltpu
from jax.sharding import Mesh, PartitionSpec as P

PANEL = 256
HALF = 128
ROWS = 16
ROW = ("zl", "core")
PLANE = ("y", "x")
COL = ("y", "x", "zh")
HIGHEST = lax.Precision.HIGHEST
SWAP = [(0, 1), (1, 0)]
F32 = jnp.float32


def member(ids, position):
    bits = sum(1 << i for i in ids)
    return (jnp.int32(bits) >> position) & 1 == 1


def panel_tree(owner):
    def branch(own):
        row = lax.axis_index(ROW)
        held, block = [owner], own
        for step in (8, 4, 2):
            pairs = [(h, h + step) for h in held if h + step < ROWS]
            moved = lax.ppermute(block, ROW, pairs)
            block = jnp.where(member([t for _, t in pairs], row), moved, block)
            held = held + [t for _, t in pairs]
        return block

    return branch


def mm(a, b, ca, cb):
    return lax.dot_general(a, b, (((ca,), (cb,)), ((), ())), precision=HIGHEST, preferred_element_type=F32)


def call(kernel, outs, *args, flops=10**9):
    cost = pl.CostEstimate(flops=flops, bytes_accessed=10**6, transcendentals=0)
    vmem = pl.BlockSpec(memory_space=pltpu.VMEM)
    return pl.pallas_call(
        kernel,
        out_shape=outs,
        in_specs=[vmem] * len(args),
        out_specs=(vmem,) * len(outs) if isinstance(outs, tuple) else vmem,
        cost_estimate=cost,
    )(*args)


def gram_kernel(flag_ref, s_ref, own_ref, moved_ref, out_ref):
    panel = jnp.where(flag_ref[...] > 0, own_ref[...], moved_ref[...])
    dims = (((1,), (1,)), ((), ()))
    gram = lax.dot_general(s_ref[...], panel, dims, preferred_element_type=F32)
    diag = lax.dot_general(panel, panel, dims, preferred_element_type=F32)
    for k in range(16):
        out_ref[k, :32, :] = gram[32 * k : 32 * k + 32]
        out_ref[k, 32:, :] = diag[16 * k : 16 * k + 16]


def rsqrt(v):
    r = lax.rsqrt(v)
    return r * (1.5 - 0.5 * v * r * r)


def fill(v):
    return jnp.broadcast_to(v, (8, HALF))


GROUPS = HALF // 8


def eliminate(a, e, out_ref, first, last):
    sub = lax.broadcasted_iota(jnp.int32, (8, HALF), 0)
    for g in range(first, last):
        rows_a, rows_e = a[g], e[g]
        columns = [fill(rows_a[:, 8 * g + j : 8 * g + j + 1]) for j in range(8)]
        for s in range(8):
            pivot = fill(columns[s][s : s + 1])
            scale = 1.0 / pivot
            row_a, row_e = fill(rows_a[s : s + 1]), fill(rows_e[s : s + 1])
            k = 8 * g + s
            out_ref[k : k + 1, :] = (row_e * rsqrt(pivot))[:1]
            weight = jnp.where(sub == s, 1.0 - scale, columns[s] * scale)
            rows_a = rows_a - weight * row_a
            rows_e = rows_e - weight * row_e
            for j in range(s + 1, 8):
                columns[j] = columns[j] - weight * fill(columns[j][s : s + 1])
        solved_a = [fill(rows_a[t : t + 1]) for t in range(8)]
        solved_e = [fill(rows_e[t : t + 1]) for t in range(8)]
        for h in range(g + 1, GROUPS):
            below = [fill(a[h][:, 8 * g + t : 8 * g + t + 1]) for t in range(8)]
            a[h] = a[h] - sum(below[t] * solved_a[t] for t in range(8))
            e[h] = e[h] - sum(below[t] * solved_e[t] for t in range(8))


def split(v):
    return [v[8 * g : 8 * g + 8] for g in range(GROUPS)]


def start_block(d_ref, after_ref, a_ref, e_ref, m_ref):
    sub = lax.broadcasted_iota(jnp.int32, (8, HALF), 0)
    lane = lax.broadcasted_iota(jnp.int32, (8, HALF), 1)
    a, e = split(d_ref[...]), [jnp.where(lane == sub + 8 * g, 1.0, 0.0) for g in range(GROUPS)]
    eliminate(a, e, m_ref, 0, GROUPS // 2)
    for g in range(GROUPS // 2, GROUPS):
        a_ref[8 * g : 8 * g + 8, :] = a[g]
        e_ref[8 * g : 8 * g + 8, :] = e[g]


def end_block(a_ref, e_ref, m_in, m_ref):
    m_ref[: HALF // 2, :] = m_in[: HALF // 2, :]
    eliminate(split(a_ref[...]), split(e_ref[...]), m_ref, GROUPS // 2, GROUPS)
    return m_ref[...]


def end_upper(a_ref, e_ref, m_in, d10_ref, d11_ref, after_ref, m_ref, x_ref, d_ref):
    m = end_block(a_ref, e_ref, m_in, m_ref)
    low = mm(d10_ref[...], m, 1, 1)
    d_ref[...] = d11_ref[...] - mm(low, low, 1, 1)
    x_ref[...] = mm(low, m, 1, 0)


def end_lower(a_ref, e_ref, m_in, m00_ref, x_ref, after_ref, out_ref, m_ref):
    m = end_block(a_ref, e_ref, m_in, m_ref)
    out_ref[:HALF, :HALF] = m00_ref[...]
    out_ref[:HALF, HALF:] = jnp.zeros((HALF, HALF), F32)
    out_ref[HALF:, HALF:] = m
    out_ref[HALF:, :HALF] = -mm(m, x_ref[...], 1, 0)


SQUARE = jax.ShapeDtypeStruct((HALF, HALF), F32)
FULL = jax.ShapeDtypeStruct((PANEL, PANEL), F32)


def window_and_inverse(cut, source, diag):
    zl, core = lax.axis_index("zl"), lax.axis_index("core")
    rows = cut.shape[0] // 2
    halves = cut.reshape(2, rows, PANEL)
    mine = jnp.where(core == 0, halves[0], halves[1])
    other = jnp.where(core == 0, halves[1], halves[0])

    def cross(block, step):
        moved = lax.ppermute(block, "zl", [(i, i ^ step) for i in range(8)])
        return jnp.where((zl ^ (source >> 1)) & step != 0, moved, block)

    token = lambda v: v[:8, :HALF]
    block = jnp.where(core == (source & 1), mine, lax.ppermute(other, "core", SWAP))
    a, e, m = call(start_block, (SQUARE,) * 3, diag[:HALF, :HALF], token(diag))
    far = cross(block, 4)
    m00, x, d11 = call(end_upper, (SQUARE,) * 3, a, e, m, diag[HALF:, :HALF], diag[HALF:, HALF:], token(block))
    mid = cross(far, 2)
    a, e, m = call(start_block, (SQUARE,) * 3, d11, token(far))
    near = cross(mid, 1)
    inverse = call(end_lower, (FULL, SQUARE), a, e, m, m00, x, token(mid))[0]
    moved = lax.ppermute(near, "core", SWAP)
    return jnp.where(core == 0, jnp.concatenate([near, moved]), jnp.concatenate([moved, near])), inverse


def local(signatures, trailing, ridge, panel_index):
    rows_dev, tile_cols = signatures.shape[0], trailing.shape[1]
    row, col = lax.axis_index(ROW), lax.axis_index(COL)
    core = lax.axis_index("core")
    x, y, zh = lax.axis_index("x"), lax.axis_index("y"), lax.axis_index("zh")
    index = panel_index[0]
    panel_start = index * PANEL
    owner = index >> 1
    own = lax.dynamic_slice_in_dim(signatures, panel_start & (rows_dev - 1), PANEL, 0)
    panel = lax.switch(owner, [panel_tree(o) for o in range(8)], own)
    moved = lax.ppermute(panel, "core", SWAP)
    flag = jnp.full((1, 1), core == (owner & 1), jnp.int32)
    parts = call(gram_kernel, jax.ShapeDtypeStruct((16, 48, PANEL), F32), flag, signatures, panel, moved)
    parts = lax.all_to_all(parts, PLANE, 0, 0, tiled=True)
    piece = jnp.sum(parts, axis=0)
    piece = piece + lax.ppermute(piece, "zh", SWAP)
    pieces = lax.all_to_all(jnp.broadcast_to(piece[None], parts.shape), PLANE, 0, 0, tiled=True)

    cut_start = 8 * ((index + 1 + x) & 1) + 4 * zh
    cut = lax.dynamic_slice_in_dim(pieces, cut_start, 4, 0)[:, :32].reshape(tile_cols, PANEL)
    diag = pieces[:, 32:].reshape(PANEL, PANEL)
    eye = jnp.eye(PANEL, dtype=F32)
    diag = jnp.where(row >= owner, diag + ridge[0] * eye, eye)
    cut, inverse = window_and_inverse(cut, 2 * y + ((index + 1 + x) >> 1), diag)

    gram = pieces[:, :32].reshape(rows_dev, PANEL)
    row_ids = row * rows_dev + lax.broadcasted_iota(jnp.int32, gram.shape, 0)
    col_ids = panel_start + lax.broadcasted_iota(jnp.int32, gram.shape, 1)
    gram = gram + jnp.where(row_ids == col_ids, ridge[0], 0.0)
    factor = jnp.where(row_ids >= panel_start, mm(gram, inverse, 1, 1), 0.0)
    window = jnp.where(row >= owner, mm(cut, inverse, 1, 1), 0.0)
    updated = trailing - mm(factor, window, 1, 1)
    return lax.dynamic_slice_in_dim(factor, col * 16, 16, 0), updated


def solution(mesh):
    names = (*ROW, *COL)
    inner = Mesh(mesh.devices.reshape(8, 2, 4, 4, 2), names)
    placed = (P(ROW, COL), P(ROW, COL), P(), P())
    return jax.shard_map(
        local,
        mesh=inner,
        in_specs=placed,
        out_specs=(P(names, None), P(ROW, COL)),
        check_vma=False,
    )
```

```python
import jax
import jax.numpy as jnp
from jax import lax
from jax.experimental import pallas as pl
from jax.experimental.pallas import tpu as pltpu
from jax.sharding import Mesh, PartitionSpec as P

PANEL = 256
HALF = 128
ROWS = 16
ROW = ("zl", "core")
PLANE = ("y", "x")
COL = ("y", "x", "zh")
HIGHEST = lax.Precision.HIGHEST
SWAP = [(0, 1), (1, 0)]
F32 = jnp.float32


def panel_tree(first):
    def branch(*pieces):
        zl = lax.axis_index("zl")
        far, back, on = first + 4, first + 2, first + 6
        last = [(i, i + 1) for i in range(first & 1, 7, 2)]
        out = []
        for piece in pieces:
            moved = lax.ppermute(piece, "zl", [(first, far)])
            piece = jnp.where(zl == far, moved, piece)
            moved = lax.ppermute(piece, "zl", [(far, back)])
            if on < 8:
                onward = lax.ppermute(piece, "zl", [(far, on)])
                piece = jnp.where(zl == on, onward, piece)
            piece = jnp.where(zl == back, moved, piece)
            moved = lax.ppermute(piece, "zl", last)
            piece = jnp.where((zl - first) & 1 == 1, moved, piece)
            out.append(lax.all_gather(piece, "core"))
        return out

    return branch


def mm(a, b, ca, cb):
    return lax.dot_general(a, b, (((ca,), (cb,)), ((), ())), precision=HIGHEST, preferred_element_type=F32)


def call(kernel, outs, *args, flops=10**9, room=4 << 20):
    cost = pl.CostEstimate(flops=flops, bytes_accessed=10**6, transcendentals=0)
    vmem = pl.BlockSpec(memory_space=pltpu.VMEM)
    return pl.pallas_call(
        kernel,
        out_shape=outs,
        in_specs=[vmem] * len(args),
        out_specs=(vmem,) * len(outs) if isinstance(outs, tuple) else vmem,
        cost_estimate=cost,
        compiler_params=pltpu.CompilerParams(vmem_limit_bytes=room),
    )(*args)


def gram_kernel(core_ref, s_ref, low_ref, high_ref, out_ref):
    halves = [jnp.concatenate([low_ref[i], high_ref[i]]) for i in range(2)]
    half = jnp.where(core_ref[...] == 0, halves[0], halves[1])
    panel = jnp.concatenate(halves)
    dims = (((1,), (1,)), ((), ()))
    gram = lax.dot_general(s_ref[...], panel, dims, preferred_element_type=F32)
    diag = lax.dot_general(half, panel, dims, preferred_element_type=F32)
    for k in range(16):
        out_ref[k, :32, :] = gram[32 * k : 32 * k + 32]
        out_ref[k, 32:, :] = diag[8 * k : 8 * k + 8]


def rsqrt(v):
    r = lax.rsqrt(v)
    return r * (1.5 - 0.5 * v * r * r)


def fill(v):
    return jnp.broadcast_to(v, (8, HALF))


GROUPS = HALF // 8


def eliminate(a, e, out_ref, first, last):
    sub = lax.broadcasted_iota(jnp.int32, (8, HALF), 0)
    for g in range(first, last):
        rows_a, rows_e = a[g], e[g]
        columns = [fill(rows_a[:, 8 * g + j : 8 * g + j + 1]) for j in range(8)]
        for s in range(8):
            pivot = fill(columns[s][s : s + 1])
            scale = 1.0 / pivot
            row_a, row_e = fill(rows_a[s : s + 1]), fill(rows_e[s : s + 1])
            k = 8 * g + s
            out_ref[k : k + 1, :] = (row_e * rsqrt(pivot))[:1]
            weight = jnp.where(sub == s, 1.0 - scale, columns[s] * scale)
            rows_a = rows_a - weight * row_a
            rows_e = rows_e - weight * row_e
            for j in range(s + 1, 8):
                columns[j] = columns[j] - weight * fill(columns[j][s : s + 1])
        solved_a = [fill(rows_a[t : t + 1]) for t in range(8)]
        solved_e = [fill(rows_e[t : t + 1]) for t in range(8)]
        for h in range(g + 1, GROUPS):
            below = [fill(a[h][:, 8 * g + t : 8 * g + t + 1]) for t in range(8)]
            a[h] = a[h] - sum(below[t] * solved_a[t] for t in range(8))
            e[h] = e[h] - sum(below[t] * solved_e[t] for t in range(8))


def split(v):
    return [v[8 * g : 8 * g + 8] for g in range(GROUPS)]


def start_block(d_ref, after_ref, a_ref, e_ref, m_ref):
    sub = lax.broadcasted_iota(jnp.int32, (8, HALF), 0)
    lane = lax.broadcasted_iota(jnp.int32, (8, HALF), 1)
    a, e = split(d_ref[...]), [jnp.where(lane == sub + 8 * g, 1.0, 0.0) for g in range(GROUPS)]
    eliminate(a, e, m_ref, 0, GROUPS // 2)
    for g in range(GROUPS // 2, GROUPS):
        a_ref[8 * g : 8 * g + 8, :] = a[g]
        e_ref[8 * g : 8 * g + 8, :] = e[g]


def end_block(a_ref, e_ref, m_in, m_ref):
    m_ref[: HALF // 2, :] = m_in[: HALF // 2, :]
    eliminate(split(a_ref[...]), split(e_ref[...]), m_ref, GROUPS // 2, GROUPS)
    return m_ref[...]


def end_upper(a_ref, e_ref, m_in, d10_ref, d11_ref, after_ref, m_ref, x_ref, d_ref):
    m = end_block(a_ref, e_ref, m_in, m_ref)
    low = mm(d10_ref[...], m, 1, 1)
    d_ref[...] = d11_ref[...] - mm(low, low, 1, 1)
    x_ref[...] = mm(low, m, 1, 0)


def end_lower(a_ref, e_ref, m_in, m00_ref, x_ref, after_ref, out_ref, m_ref):
    m = end_block(a_ref, e_ref, m_in, m_ref)
    out_ref[:HALF, :HALF] = m00_ref[...]
    out_ref[:HALF, HALF:] = jnp.zeros((HALF, HALF), F32)
    out_ref[HALF:, HALF:] = m
    out_ref[HALF:, :HALF] = -mm(m, x_ref[...], 1, 0)


SQUARE = jax.ShapeDtypeStruct((HALF, HALF), F32)
FULL = jax.ShapeDtypeStruct((PANEL, PANEL), F32)


def window_and_inverse(cut, source, diag_half, prepare):
    zl, core = lax.axis_index("zl"), lax.axis_index("core")
    rows = cut.shape[0] // 2
    halves = cut.reshape(2, rows, PANEL)
    mine = jnp.where(core == 0, halves[0], halves[1])
    other = jnp.where(core == 0, halves[1], halves[0])

    def cross(block, step):
        moved = lax.ppermute(block, "zl", [(i, i ^ step) for i in range(8)])
        return jnp.where((zl ^ (source >> 1)) & step != 0, moved, block)

    token = lambda v: v[:8, :HALF]
    both = lax.all_gather(jnp.concatenate([diag_half, other]), "core")
    diag = prepare(both[:, :HALF].reshape(PANEL, PANEL))
    moved = jnp.where(core == 0, both[1, HALF:], both[0, HALF:])
    block = jnp.where(core == (source & 1), mine, moved)
    far = cross(block, 4)
    a, e, m = call(start_block, (SQUARE,) * 3, diag[:HALF, :HALF], token(block))
    m00, x, d11 = call(end_upper, (SQUARE,) * 3, a, e, m, diag[HALF:, :HALF], diag[HALF:, HALF:], token(block))
    a, e, m = call(start_block, (SQUARE,) * 3, d11, token(block))
    mid = cross(far, 2)
    inverse = call(end_lower, (FULL, SQUARE), a, e, m, m00, x, token(far))[0]
    four = lax.all_gather(mid, ROW, axis_index_groups=[[i, i + 1, i + 2, i + 3] for i in range(0, ROWS, 4)])
    return jnp.where((source >> 1) & 1 == 0, four[:2], four[2:]).reshape(cut.shape), inverse


def local(signatures, trailing, ridge, panel_index):
    rows_dev, tile_cols = signatures.shape[0], trailing.shape[1]
    row, col = lax.axis_index(ROW), lax.axis_index(COL)
    core = lax.axis_index("core")
    x, y, zh = lax.axis_index("x"), lax.axis_index("y"), lax.axis_index("zh")
    index = panel_index[0]
    panel_start = index * PANEL
    owner = index >> 1
    offset = panel_start & (rows_dev - 1)
    mine = lax.dynamic_slice_in_dim(signatures, offset + HALF * core, HALF, 0)
    other = lax.dynamic_slice_in_dim(signatures, offset + HALF * (1 - core), HALF, 0)
    half = jnp.where(core == (owner & 1), mine, lax.ppermute(other, "core", SWAP))
    low, high = lax.switch(owner >> 1, [panel_tree(i) for i in range(4)], half[: HALF // 2], half[HALF // 2 :])
    parts = call(
        gram_kernel,
        jax.ShapeDtypeStruct((16, 40, PANEL), F32),
        jnp.full((1, 1), core, jnp.int32),
        signatures,
        low,
        high,
        room=16 << 20,
    )
    parts = lax.all_to_all(parts, PLANE, 0, 0, tiled=True)
    piece = jnp.sum(lax.all_gather(jnp.sum(parts, axis=0), "zh"), axis=0)
    pieces = lax.all_to_all(jnp.broadcast_to(piece[None], parts.shape), PLANE, 0, 0, tiled=True)

    cut_start = 8 * ((index + 1 + x) & 1) + 4 * zh
    cut = lax.dynamic_slice_in_dim(pieces, cut_start, 4, 0)[:, :32].reshape(tile_cols, PANEL)
    eye = jnp.eye(PANEL, dtype=F32)
    prepare = lambda diag: jnp.where(row >= owner, diag + ridge[0] * eye, eye)
    source = 2 * y + ((index + 1 + x) >> 1)
    cut, inverse = window_and_inverse(cut, source, pieces[:, 32:].reshape(HALF, PANEL), prepare)

    gram = pieces[:, :32].reshape(rows_dev, PANEL)
    row_ids = row * rows_dev + lax.broadcasted_iota(jnp.int32, gram.shape, 0)
    col_ids = panel_start + lax.broadcasted_iota(jnp.int32, gram.shape, 1)
    gram = gram + jnp.where(row_ids == col_ids, ridge[0], 0.0)
    factor = jnp.where(row_ids >= panel_start, mm(gram, inverse, 1, 1), 0.0)
    window = jnp.where(row >= owner, mm(cut, inverse, 1, 1), 0.0)
    updated = trailing - mm(factor, window, 1, 1)
    return lax.dynamic_slice_in_dim(factor, col * 16, 16, 0), updated


def solution(mesh):
    names = (*ROW, *COL)
    inner = Mesh(mesh.devices.reshape(8, 2, 4, 4, 2), names)
    placed = (P(ROW, COL), P(ROW, COL), P(), P())
    return jax.shard_map(
        local,
        mesh=inner,
        in_specs=placed,
        out_specs=(P(names, None), P(ROW, COL)),
        check_vma=False,
    )
```

```python
import jax
import jax.numpy as jnp
from jax import lax
from jax.experimental import pallas as pl
from jax.experimental.pallas import tpu as pltpu
from jax.sharding import Mesh, PartitionSpec as P

PANEL = 256
HALF = 128
ROWS = 16
ROW = ("zl", "core")
PLANE = ("y", "x")
COL = ("y", "x", "zh")
HIGHEST = lax.Precision.HIGHEST
SWAP = [(0, 1), (1, 0)]
F32 = jnp.float32


def panel_tree(first):
    def branch(*pieces):
        zl = lax.axis_index("zl")
        far, back, on = first + 4, first + 2, first + 6
        last = [(i, i + 1) for i in range(first & 1, 7, 2)]
        out = []
        for piece in pieces:
            moved = lax.ppermute(piece, "zl", [(first, far)])
            piece = jnp.where(zl == far, moved, piece)
            moved = lax.ppermute(piece, "zl", [(far, back)])
            if on < 8:
                onward = lax.ppermute(piece, "zl", [(far, on)])
                piece = jnp.where(zl == on, onward, piece)
            piece = jnp.where(zl == back, moved, piece)
            moved = lax.ppermute(piece, "zl", last)
            piece = jnp.where((zl - first) & 1 == 1, moved, piece)
            out.append(lax.all_gather(piece, "core"))
        return out

    return branch


def mm(a, b, ca, cb):
    return lax.dot_general(a, b, (((ca,), (cb,)), ((), ())), precision=HIGHEST, preferred_element_type=F32)


def call(kernel, outs, *args, flops=10**9, room=4 << 20):
    cost = pl.CostEstimate(flops=flops, bytes_accessed=10**6, transcendentals=0)
    vmem = pl.BlockSpec(memory_space=pltpu.VMEM)
    return pl.pallas_call(
        kernel,
        out_shape=outs,
        in_specs=[vmem] * len(args),
        out_specs=(vmem,) * len(outs) if isinstance(outs, tuple) else vmem,
        cost_estimate=cost,
        compiler_params=pltpu.CompilerParams(vmem_limit_bytes=room),
    )(*args)


def gram_kernel(core_ref, s_ref, low_ref, high_ref, out_ref):
    halves = [jnp.concatenate([low_ref[i], high_ref[i]]) for i in range(2)]
    half = jnp.where(core_ref[...] == 0, halves[0], halves[1])
    panel = jnp.concatenate(halves)
    dims = (((1,), (1,)), ((), ()))
    gram = lax.dot_general(s_ref[...], panel, dims, preferred_element_type=F32)
    diag = lax.dot_general(half, panel, dims, preferred_element_type=F32)
    for k in range(16):
        out_ref[k, :32, :] = gram[32 * k : 32 * k + 32]
        out_ref[k, 32:, :] = diag[8 * k : 8 * k + 8]


def rsqrt(v):
    r = lax.rsqrt(v)
    return r * (1.5 - 0.5 * v * r * r)


def fill(v):
    return jnp.broadcast_to(v, (8, HALF))


GROUPS = HALF // 8


def eliminate(a, e, out_ref, first, last):
    sub = lax.broadcasted_iota(jnp.int32, (8, HALF), 0)
    for g in range(first, last):
        rows_a, rows_e = a[g], e[g]
        columns = [fill(rows_a[:, 8 * g + j : 8 * g + j + 1]) for j in range(8)]
        for s in range(8):
            pivot = fill(columns[s][s : s + 1])
            scale = 1.0 / pivot
            row_a, row_e = fill(rows_a[s : s + 1]), fill(rows_e[s : s + 1])
            k = 8 * g + s
            out_ref[k : k + 1, :] = (row_e * rsqrt(pivot))[:1]
            weight = jnp.where(sub == s, 1.0 - scale, columns[s] * scale)
            rows_a = rows_a - weight * row_a
            rows_e = rows_e - weight * row_e
            for j in range(s + 1, 8):
                columns[j] = columns[j] - weight * fill(columns[j][s : s + 1])
        solved_a = [fill(rows_a[t : t + 1]) for t in range(8)]
        solved_e = [fill(rows_e[t : t + 1]) for t in range(8)]
        for h in range(g + 1, GROUPS):
            below = [fill(a[h][:, 8 * g + t : 8 * g + t + 1]) for t in range(8)]
            a[h] = a[h] - sum(below[t] * solved_a[t] for t in range(8))
            e[h] = e[h] - sum(below[t] * solved_e[t] for t in range(8))


def split(v):
    return [v[8 * g : 8 * g + 8] for g in range(GROUPS)]


def start_block(d_ref, after_ref, a_ref, e_ref, m_ref):
    sub = lax.broadcasted_iota(jnp.int32, (8, HALF), 0)
    lane = lax.broadcasted_iota(jnp.int32, (8, HALF), 1)
    a, e = split(d_ref[...]), [jnp.where(lane == sub + 8 * g, 1.0, 0.0) for g in range(GROUPS)]
    eliminate(a, e, m_ref, 0, GROUPS // 2)
    for g in range(GROUPS // 2, GROUPS):
        a_ref[8 * g : 8 * g + 8, :] = a[g]
        e_ref[8 * g : 8 * g + 8, :] = e[g]


def end_block(a_ref, e_ref, m_in, m_ref):
    m_ref[: HALF // 2, :] = m_in[: HALF // 2, :]
    eliminate(split(a_ref[...]), split(e_ref[...]), m_ref, GROUPS // 2, GROUPS)
    return m_ref[...]


def end_upper(a_ref, e_ref, m_in, d10_ref, d11_ref, after_ref, m_ref, x_ref, d_ref):
    m = end_block(a_ref, e_ref, m_in, m_ref)
    low = mm(d10_ref[...], m, 1, 1)
    d_ref[...] = d11_ref[...] - mm(low, low, 1, 1)
    x_ref[...] = mm(low, m, 1, 0)


def end_lower(a_ref, e_ref, m_in, m00_ref, x_ref, after_ref, out_ref, m_ref):
    m = end_block(a_ref, e_ref, m_in, m_ref)
    out_ref[:HALF, :HALF] = m00_ref[...]
    out_ref[:HALF, HALF:] = jnp.zeros((HALF, HALF), F32)
    out_ref[HALF:, HALF:] = m
    out_ref[HALF:, :HALF] = -mm(m, x_ref[...], 1, 0)


SQUARE = jax.ShapeDtypeStruct((HALF, HALF), F32)
FULL = jax.ShapeDtypeStruct((PANEL, PANEL), F32)


def window_and_inverse(cut, source, diag_half, prepare):
    zl, core = lax.axis_index("zl"), lax.axis_index("core")
    rows = cut.shape[0] // 2
    halves = cut.reshape(2, rows, PANEL)
    mine = jnp.where(core == 0, halves[0], halves[1])
    other = jnp.where(core == 0, halves[1], halves[0])

    def cross(block, step):
        moved = lax.ppermute(block, "zl", [(i, i ^ step) for i in range(8)])
        return jnp.where((zl ^ (source >> 1)) & step != 0, moved, block)

    token = lambda v: v[:8, :HALF]
    both = lax.all_gather(jnp.concatenate([diag_half, other]), "core")
    diag = prepare(both[:, :HALF].reshape(PANEL, PANEL))
    moved = jnp.where(core == 0, both[1, HALF:], both[0, HALF:])
    block = jnp.where(core == (source & 1), mine, moved)
    far = cross(block, 4)
    a, e, m = call(start_block, (SQUARE,) * 3, diag[:HALF, :HALF], token(block))
    m00, x, d11 = call(end_upper, (SQUARE,) * 3, a, e, m, diag[HALF:, :HALF], diag[HALF:, HALF:], token(block))
    a, e, m = call(start_block, (SQUARE,) * 3, d11, token(block))
    mid = cross(far, 2)
    inverse = call(end_lower, (FULL, SQUARE), a, e, m, m00, x, token(far))[0]
    four = lax.all_gather(mid, ROW, axis_index_groups=[[i, i + 1, i + 2, i + 3] for i in range(0, ROWS, 4)])
    return jnp.where((source >> 1) & 1 == 0, four[:2], four[2:]).reshape(cut.shape), inverse


def local(signatures, trailing, ridge, panel_index):
    rows_dev, tile_cols = signatures.shape[0], trailing.shape[1]
    row, col = lax.axis_index(ROW), lax.axis_index(COL)
    core = lax.axis_index("core")
    x, y, zh = lax.axis_index("x"), lax.axis_index("y"), lax.axis_index("zh")
    index = panel_index[0]
    panel_start = index * PANEL
    owner = index >> 1
    offset = panel_start & (rows_dev - 1)
    mine = lax.dynamic_slice_in_dim(signatures, offset + HALF * core, HALF, 0)
    other = lax.dynamic_slice_in_dim(signatures, offset + HALF * (1 - core), HALF, 0)
    swapped = lax.all_gather(other, "core")
    half = jnp.where(core == (owner & 1), mine, jnp.where(core == 0, swapped[1], swapped[0]))
    low, high = lax.switch(owner >> 1, [panel_tree(i) for i in range(4)], half[: HALF // 2], half[HALF // 2 :])
    parts = call(
        gram_kernel,
        jax.ShapeDtypeStruct((16, 40, PANEL), F32),
        jnp.full((1, 1), core, jnp.int32),
        signatures,
        low,
        high,
        room=16 << 20,
    )
    parts = lax.all_to_all(parts, PLANE, 0, 0, tiled=True)
    piece = jnp.sum(lax.all_gather(jnp.sum(parts, axis=0), "zh"), axis=0)
    pieces = lax.all_to_all(jnp.broadcast_to(piece[None], parts.shape), PLANE, 0, 0, tiled=True)

    cut_start = 8 * ((index + 1 + x) & 1) + 4 * zh
    cut = lax.dynamic_slice_in_dim(pieces, cut_start, 4, 0)[:, :32].reshape(tile_cols, PANEL)
    eye = jnp.eye(PANEL, dtype=F32)
    prepare = lambda diag: jnp.where(row >= owner, diag + ridge[0] * eye, eye)
    source = 2 * y + ((index + 1 + x) >> 1)
    cut, inverse = window_and_inverse(cut, source, pieces[:, 32:].reshape(HALF, PANEL), prepare)

    gram = pieces[:, :32].reshape(rows_dev, PANEL)
    row_ids = row * rows_dev + lax.broadcasted_iota(jnp.int32, gram.shape, 0)
    col_ids = panel_start + lax.broadcasted_iota(jnp.int32, gram.shape, 1)
    gram = gram + jnp.where(row_ids == col_ids, ridge[0], 0.0)
    factor = jnp.where(row_ids >= panel_start, mm(gram, inverse, 1, 1), 0.0)
    window = jnp.where(row >= owner, mm(cut, inverse, 1, 1), 0.0)
    updated = trailing - mm(factor, window, 1, 1)
    return lax.dynamic_slice_in_dim(factor, col * 16, 16, 0), updated


def solution(mesh):
    names = (*ROW, *COL)
    inner = Mesh(mesh.devices.reshape(8, 2, 4, 4, 2), names)
    placed = (P(ROW, COL), P(ROW, COL), P(), P())
    return jax.shard_map(
        local,
        mesh=inner,
        in_specs=placed,
        out_specs=(P(names, None), P(ROW, COL)),
        check_vma=False,
    )
```

```python
import jax
import jax.numpy as jnp
from jax import lax
from jax.experimental import pallas as pl
from jax.experimental.pallas import tpu as pltpu
from jax.sharding import Mesh, PartitionSpec as P

PANEL = 256
HALF = 128
ROWS = 16
ROW = ("zl", "core")
PLANE = ("y", "x")
COL = ("y", "x", "zh")
HIGHEST = lax.Precision.HIGHEST
SWAP = [(0, 1), (1, 0)]
F32 = jnp.float32


def panel_tree(first):
    def branch(*pieces):
        zl = lax.axis_index("zl")
        far, back, on = first + 4, first + 2, first + 6
        last = [(i, i + 1) for i in range(first & 1, 7, 2)]
        out = []
        for piece in pieces:
            moved = lax.ppermute(piece, "zl", [(first, far)])
            piece = jnp.where(zl == far, moved, piece)
            moved = lax.ppermute(piece, "zl", [(far, back)])
            if on < 8:
                onward = lax.ppermute(piece, "zl", [(far, on)])
                piece = jnp.where(zl == on, onward, piece)
            piece = jnp.where(zl == back, moved, piece)
            moved = lax.ppermute(piece, "zl", last)
            piece = jnp.where((zl - first) & 1 == 1, moved, piece)
            out.append(lax.all_gather(piece, "core"))
        return out

    return branch


def mm(a, b, ca, cb):
    return lax.dot_general(a, b, (((ca,), (cb,)), ((), ())), precision=HIGHEST, preferred_element_type=F32)


def call(kernel, outs, *args, flops=10**9, room=4 << 20):
    cost = pl.CostEstimate(flops=flops, bytes_accessed=10**6, transcendentals=0)
    vmem = pl.BlockSpec(memory_space=pltpu.VMEM)
    return pl.pallas_call(
        kernel,
        out_shape=outs,
        in_specs=[vmem] * len(args),
        out_specs=(vmem,) * len(outs) if isinstance(outs, tuple) else vmem,
        cost_estimate=cost,
        compiler_params=pltpu.CompilerParams(vmem_limit_bytes=room),
    )(*args)


def gram_kernel(core_ref, s_ref, low_ref, high_ref, out_ref):
    halves = [jnp.concatenate([low_ref[i], high_ref[i]]) for i in range(2)]
    half = jnp.where(core_ref[...] == 0, halves[0], halves[1])
    panel = jnp.concatenate(halves)
    dims = (((1,), (1,)), ((), ()))
    gram = lax.dot_general(s_ref[...], panel, dims, preferred_element_type=F32)
    diag = lax.dot_general(half, panel, dims, preferred_element_type=F32)
    for k in range(16):
        out_ref[k, :32, :] = gram[32 * k : 32 * k + 32]
        out_ref[k, 32:, :] = diag[8 * k : 8 * k + 8]


def rsqrt(v):
    r = lax.rsqrt(v)
    return r * (1.5 - 0.5 * v * r * r)


def fill(v):
    return jnp.broadcast_to(v, (8, HALF))


GROUPS = HALF // 8


def eliminate(a, e, out_ref, first, last):
    sub = lax.broadcasted_iota(jnp.int32, (8, HALF), 0)
    for g in range(first, last):
        rows_a, rows_e = a[g], e[g]
        columns = [fill(rows_a[:, 8 * g + j : 8 * g + j + 1]) for j in range(8)]
        for s in range(8):
            pivot = fill(columns[s][s : s + 1])
            scale = 1.0 / pivot
            row_a, row_e = fill(rows_a[s : s + 1]), fill(rows_e[s : s + 1])
            k = 8 * g + s
            out_ref[k : k + 1, :] = (row_e * rsqrt(pivot))[:1]
            weight = jnp.where(sub == s, 1.0 - scale, columns[s] * scale)
            rows_a = rows_a - weight * row_a
            rows_e = rows_e - weight * row_e
            for j in range(s + 1, 8):
                columns[j] = columns[j] - weight * fill(columns[j][s : s + 1])
        solved_a = [fill(rows_a[t : t + 1]) for t in range(8)]
        solved_e = [fill(rows_e[t : t + 1]) for t in range(8)]
        for h in range(g + 1, GROUPS):
            below = [fill(a[h][:, 8 * g + t : 8 * g + t + 1]) for t in range(8)]
            a[h] = a[h] - sum(below[t] * solved_a[t] for t in range(8))
            e[h] = e[h] - sum(below[t] * solved_e[t] for t in range(8))


def split(v):
    return [v[8 * g : 8 * g + 8] for g in range(GROUPS)]


def start_block(d_ref, after_ref, a_ref, e_ref, m_ref):
    sub = lax.broadcasted_iota(jnp.int32, (8, HALF), 0)
    lane = lax.broadcasted_iota(jnp.int32, (8, HALF), 1)
    a, e = split(d_ref[...]), [jnp.where(lane == sub + 8 * g, 1.0, 0.0) for g in range(GROUPS)]
    eliminate(a, e, m_ref, 0, GROUPS // 2)
    for g in range(GROUPS // 2, GROUPS):
        a_ref[8 * g : 8 * g + 8, :] = a[g]
        e_ref[8 * g : 8 * g + 8, :] = e[g]


def end_block(a_ref, e_ref, m_in, m_ref):
    m_ref[: HALF // 2, :] = m_in[: HALF // 2, :]
    eliminate(split(a_ref[...]), split(e_ref[...]), m_ref, GROUPS // 2, GROUPS)
    return m_ref[...]


def end_upper(a_ref, e_ref, m_in, d10_ref, d11_ref, after_ref, m_ref, x_ref, d_ref):
    m = end_block(a_ref, e_ref, m_in, m_ref)
    low = mm(d10_ref[...], m, 1, 1)
    d_ref[...] = d11_ref[...] - mm(low, low, 1, 1)
    x_ref[...] = mm(low, m, 1, 0)


def end_lower(a_ref, e_ref, m_in, m00_ref, x_ref, after_ref, out_ref, m_ref):
    m = end_block(a_ref, e_ref, m_in, m_ref)
    out_ref[:HALF, :HALF] = m00_ref[...]
    out_ref[:HALF, HALF:] = jnp.zeros((HALF, HALF), F32)
    out_ref[HALF:, HALF:] = m
    out_ref[HALF:, :HALF] = -mm(m, x_ref[...], 1, 0)


SQUARE = jax.ShapeDtypeStruct((HALF, HALF), F32)
FULL = jax.ShapeDtypeStruct((PANEL, PANEL), F32)


def window_and_inverse(cut, source, diag_half, prepare):
    zl, core = lax.axis_index("zl"), lax.axis_index("core")
    rows = cut.shape[0] // 2
    halves = cut.reshape(2, rows, PANEL)
    mine = jnp.where(core == 0, halves[0], halves[1])
    other = jnp.where(core == 0, halves[1], halves[0])

    def cross(block, step):
        moved = lax.ppermute(block, "zl", [(i, i ^ step) for i in range(8)])
        return jnp.where((zl ^ (source >> 1)) & step != 0, moved, block)

    token = lambda v: v[:8, :HALF]
    both = lax.all_gather(jnp.concatenate([diag_half, other]), "core")
    diag = prepare(both[:, :HALF].reshape(PANEL, PANEL))
    moved = jnp.where(core == 0, both[1, HALF:], both[0, HALF:])
    block = jnp.where(core == (source & 1), mine, moved)
    far = cross(block, 4)
    a, e, m = call(start_block, (SQUARE,) * 3, diag[:HALF, :HALF], token(block))
    m00, x, d11 = call(end_upper, (SQUARE,) * 3, a, e, m, diag[HALF:, :HALF], diag[HALF:, HALF:], token(block))
    a, e, m = call(start_block, (SQUARE,) * 3, d11, token(block))
    mid = cross(far, 2)
    inverse = call(end_lower, (FULL, SQUARE), a, e, m, m00, x, token(far))[0]
    four = lax.all_gather(mid, ROW, axis_index_groups=[[i, i + 1, i + 2, i + 3] for i in range(0, ROWS, 4)])
    return jnp.where((source >> 1) & 1 == 0, four[:2], four[2:]).reshape(cut.shape), inverse


def local(signatures, trailing, ridge, panel_index):
    rows_dev, tile_cols = signatures.shape[0], trailing.shape[1]
    row, col = lax.axis_index(ROW), lax.axis_index(COL)
    core = lax.axis_index("core")
    x, y, zh = lax.axis_index("x"), lax.axis_index("y"), lax.axis_index("zh")
    index = panel_index[0]
    panel_start = index * PANEL
    owner = index >> 1
    offset = panel_start & (rows_dev - 1)
    mine = lax.dynamic_slice_in_dim(signatures, offset + HALF * core, HALF, 0)
    other = lax.dynamic_slice_in_dim(signatures, offset + HALF * (1 - core), HALF, 0)
    swapped = lax.all_gather(other, "core")
    half = jnp.where(core == (owner & 1), mine, jnp.where(core == 0, swapped[1], swapped[0]))
    low, high = lax.switch(owner >> 1, [panel_tree(i) for i in range(4)], half[: HALF // 2], half[HALF // 2 :])
    parts = call(
        gram_kernel,
        jax.ShapeDtypeStruct((16, 40, PANEL), F32),
        jnp.full((1, 1), core, jnp.int32),
        signatures,
        low,
        high,
        room=16 << 20,
    )
    parts = lax.all_to_all(parts, PLANE, 0, 0, tiled=True)
    piece = jnp.sum(lax.all_gather(jnp.sum(parts, axis=0), "zh"), axis=0)
    pieces = lax.all_to_all(jnp.broadcast_to(piece[None], parts.shape), PLANE, 0, 0, tiled=True)

    cut_start = 8 * ((index + 1 + x) & 1) + 4 * zh
    cut = lax.dynamic_slice_in_dim(pieces, cut_start, 4, 0)[:, :32].reshape(tile_cols, PANEL)
    eye = jnp.eye(PANEL, dtype=F32)
    prepare = lambda diag: jnp.where(row >= owner, diag + ridge[0] * eye, eye)
    source = 2 * y + ((index + 1 + x) >> 1)
    cut, inverse = window_and_inverse(cut, source, pieces[:, 32:].reshape(HALF, PANEL), prepare)

    gram = pieces[:, :32].reshape(rows_dev, PANEL)
    row_ids = row * rows_dev + lax.broadcasted_iota(jnp.int32, gram.shape, 0)
    col_ids = panel_start + lax.broadcasted_iota(jnp.int32, gram.shape, 1)
    gram = gram + jnp.where(row_ids == col_ids, ridge[0], 0.0)
    factor = jnp.where(row_ids >= panel_start, mm(gram, inverse, 1, 1), 0.0)
    solved = mm(factor, inverse, 1, 0)
    updated = trailing - mm(solved, jnp.where(row >= owner, cut, 0.0), 1, 1)
    return lax.dynamic_slice_in_dim(factor, col * 16, 16, 0), updated


def solution(mesh):
    names = (*ROW, *COL)
    inner = Mesh(mesh.devices.reshape(8, 2, 4, 4, 2), names)
    placed = (P(ROW, COL), P(ROW, COL), P(), P())
    return jax.shard_map(
        local,
        mesh=inner,
        in_specs=placed,
        out_specs=(P(names, None), P(ROW, COL)),
        check_vma=False,
    )
```
